32 devices in a mesh: mem: 4 (over z), lat: 8 (over y, x, core).
Axes of the slice: x: 2, y: 2, z: 4, core: 2. Of those that a mesh axis runs over, the one named last changes fastest.
Arguments:
- v_fine: float32 [128, 1024], P('lat'), may hold values from -6 to 6
- v_coarse: float32 [256, 256], P('lat'), may hold values from -6 to 6
- pert_fine: bfloat16 [64, 128, 1024], P('mem', 'lat'), may hold values from -6 to 6
- pert_coarse: bfloat16 [64, 256, 256], P('mem', 'lat'), may hold values from -6 to 6
- gauss_lat: bfloat16 [256, 256], replicated, may hold values from 0 to 0.5629165, as said below
- gauss_lon: bfloat16 [256, 256], replicated, may hold values from 0 to 1.0277402, as said below
Outputs:
- fine_increment: float32 [128, 1024], P('lat')
- coarse_increment: float32 [256, 256], P('lat')
The draws below stay inside these ranges and needn't reach their ends.
Inputs may be any that keep to these rules, and one draw needn't show every extreme that they name: `gauss_lat`: nonnegative entries. `gauss_lon`: nonnegative entries.
All inputs are finite; a program needn't handle non-finite values.
Results may differ from the reference program's by a relative error of at most 0.005.
Values may be sent and summed in bfloat16 or wider, within the bound.
A program may use at most 64 MiB of HBM per device.

```python
import math
import jax
import jax.numpy as jnp
from jax import lax

FLON = 1024
CLAT = 256
CLON = 256
MEMBERS = 64
FLAT = 128


def gauss_matrix(key, order, spread):
    spots = jnp.arange(order).astype(jnp.float32)
    kernel = jnp.exp(-0.5 * ((spots[:, None] - spots[None, :]) / spread) ** 2)
    rough = jax.random.uniform(key, (order, order), jnp.float32, 0.5, 1.5)
    return (kernel * rough * (3.0 / spread ** 0.5)).astype(jnp.bfloat16)


def draw_gauss_lat(key, part):
    return gauss_matrix(jax.random.fold_in(key, 11), CLAT, CLAT / 3.0)


def draw_gauss_lon(key, part):
    return gauss_matrix(jax.random.fold_in(key, 23), CLON, CLON / 10.0)


def block_levels(key, dims, cuts, low, high):
    def one(dim, parts):
        steps = jax.random.uniform(jax.random.fold_in(jax.random.fold_in(key, 6), dim), (parts,), jnp.float32, low / len(cuts), high / len(cuts))
        return jnp.repeat(jnp.exp(steps), dims[dim] // parts).reshape((-1,) + (1,) * (len(dims) - dim - 1))

    level = one(*cuts[0])
    for cut in cuts[1:]:
        level = level * one(*cut)
    return level


def bell_draw(stream_key, extent, scale, most, cuts=(), kind=jnp.bfloat16):
    drawn = scale * jax.random.normal(stream_key, extent, jnp.float32)
    if cuts:
        drawn = drawn * block_levels(stream_key, extent, cuts, -0.22, 0.18)
    return jnp.clip(drawn, -most, most).astype(kind)


def setup_inputs(seed: int = 0) -> dict:
    key_list = jax.random.split(jax.random.key(seed), 7)
    return {
        "v_fine": bell_draw(key_list[0], (FLAT, FLON), 1.0, 6.0, ((0, 8),), jnp.float32),
        "v_coarse": bell_draw(key_list[1], (CLAT, CLON), 1.0, 6.0, ((0, 8),), jnp.float32),
        "pert_fine": bell_draw(key_list[2], (MEMBERS, FLAT, FLON), 1.0, 6.0, ((0, 4), (1, 8))),
        "pert_coarse": bell_draw(key_list[3], (MEMBERS, CLAT, CLON), 1.0, 6.0, ((0, 4), (1, 8))),
        "gauss_lat": draw_gauss_lat(jax.random.fold_in(key_list[6], 71), 0),
        "gauss_lon": draw_gauss_lon(jax.random.fold_in(key_list[6], 71), 0),
    }


def fine_taps():
    return [math.exp(-(offset - 5) * (offset - 5) / 32.0) for offset in range(11)]


def reference(v_fine, v_coarse, pert_fine, pert_coarse, gauss_lat, gauss_lon):
    taps = fine_taps()

    def one_member(carry, pieces):
        fine_pert, coarse_pert = pieces
        weighted = (fine_pert.astype(jnp.float32) * v_fine).astype(jnp.bfloat16)
        padded = jnp.pad(weighted, ((5, 5), (0, 0)))
        along = jnp.zeros((FLAT, FLON), jnp.float32)
        for offset in range(11):
            along = along + taps[offset] * padded[offset:offset + FLAT].astype(jnp.float32)
        across = jnp.zeros((FLAT, FLON), jnp.float32)
        for offset in range(11):
            across = across + taps[offset] * jnp.roll(along, offset - 5, axis=1)
        fine_term = fine_pert.astype(jnp.float32) * across
        cweighted = (coarse_pert.astype(jnp.float32) * v_coarse).astype(jnp.bfloat16)
        ctrans = jnp.dot(cweighted, gauss_lon.T, preferred_element_type=jnp.float32).astype(jnp.bfloat16)
        smooth = jnp.dot(gauss_lat, ctrans, preferred_element_type=jnp.float32).astype(jnp.bfloat16)
        coarse_term = coarse_pert.astype(jnp.float32) * smooth.astype(jnp.float32)
        return (carry[0] + fine_term, carry[1] + coarse_term), None

    start = (jnp.zeros((FLAT, FLON), jnp.float32), jnp.zeros((CLAT, CLON), jnp.float32))
    (fine_total, coarse_total), _ = lax.scan(one_member, start, (pert_fine, pert_coarse))
    factor = 1.0 / (MEMBERS - 1)
    return fine_total * factor, coarse_total * factor
```

```python
import functools
import math

import jax
import jax.numpy as jnp
import numpy as np
from jax import lax
from jax.experimental import pallas as pl
from jax.experimental.pallas import tpu as pltpu
from jax.sharding import PartitionSpec as P

REACH = 5
MESH = pl.DeviceIdType.MESH
F32 = jnp.float32
BF16 = jnp.bfloat16


def extended(shard, sides, width):
    for axis, dim in sides:
        count, length = (lax.axis_size(axis), shard.shape[dim])
        up = [(i, (i + 1) % count) for i in range(count - 1)]
        down = [(j, i) for i, j in up]
        last = lax.slice_in_dim(shard, length - width, length, axis=dim)
        leading = lax.slice_in_dim(shard, 0, width, axis=dim)
        before = lax.ppermute(last, axis, up)
        after = lax.ppermute(leading, axis, down)
        shard = jnp.concatenate([before, shard, after], axis=dim)
    return shard


def fine_taps():
    return [math.exp(-(offset - 5) * (offset - 5) / 32.0) for offset in range(11)]


def general(v_fine, v_coarse, pert_fine, pert_coarse, gauss_lat, gauss_lon):
    taps = fine_taps()
    count = pert_fine.shape[0]
    members = count * lax.axis_size("mem")
    rows = pert_fine.shape[1]
    weighted = (pert_fine.astype(jnp.float32) * v_fine[None]).astype(jnp.bfloat16)
    padded = extended(weighted, (("lat", 1),), 5)
    along = taps[0] * padded[:, 0:rows].astype(jnp.float32)
    for offset in range(1, 11):
        along = along + taps[offset] * padded[:, offset : offset + rows].astype(jnp.float32)
    across = taps[0] * jnp.roll(along, -5, axis=2)
    for offset in range(1, 11):
        across = across + taps[offset] * jnp.roll(along, offset - 5, axis=2)
    fine_part = jnp.sum(pert_fine.astype(jnp.float32) * across, axis=0)
    crows = pert_coarse.shape[1]
    cwidth = pert_coarse.shape[2]
    cweighted = (pert_coarse.astype(jnp.float32) * v_coarse[None]).astype(jnp.bfloat16)
    flat_rows = cweighted.reshape(count * crows, cwidth)
    ctrans = jnp.einsum("rc,dc->rd", flat_rows, gauss_lon, preferred_element_type=jnp.float32)
    ctrans = ctrans.astype(jnp.bfloat16).reshape(count, crows, cwidth)
    band = lax.dynamic_slice_in_dim(gauss_lat, lax.axis_index("lat") * crows, crows, 0)
    smooth = jnp.einsum(
        "rj,mjc->mrc",
        band,
        lax.all_gather(ctrans, "lat", axis=1, tiled=True),
        preferred_element_type=jnp.float32,
    ).astype(jnp.bfloat16)
    coarse_part = jnp.sum(pert_coarse.astype(jnp.float32) * smooth.astype(jnp.float32), axis=0)
    fine_total, coarse_total = lax.psum((fine_part, coarse_part), "mem")
    factor = 1.0 / (members - 1)
    return (fine_total * factor, coarse_total * factor)


def tap(d):
    return np.where(np.abs(d) <= REACH, np.exp(-(d * d) / 32.0), 0.0)


def constants(count, rows, block):
    member = np.repeat(np.arange(count), rows)
    row = np.tile(np.arange(rows), count)
    own = (member[:, None] == member[None, :]) * tap(row[:, None] - row[None, :])
    edge_member = np.tile(np.arange(count), REACH)
    step = np.repeat(np.arange(REACH), count)
    same = edge_member[:, None] == member[None, :]
    to_next = same * tap(row[None, :] - (rows + step)[:, None])
    to_before = same * tap(row[None, :] - (step - REACH)[:, None])
    first = same * (row[None, :] == step[:, None])
    last = same * (row[None, :] == (rows - REACH + step)[:, None])
    half = block // 2
    lon = tap(np.arange(2 * block)[:, None] - half - np.arange(block)[None, :])
    spread = np.concatenate([to_next, to_before], 0)
    pick = np.concatenate([first, last], 0)
    return [jnp.asarray(a, BF16) for a in (own, spread, pick, lon)]


def dot(a, b):
    return jnp.dot(a, b, preferred_element_type=F32)


def kernel(
    bands, groups, block, factor,
    v_fine, v_coarse, pert_fine, pert_coarse, gauss_lat, gauss_lon, own_m, spread_m, pick_m, lon_m,
    out_fine, out_coarse,
    vf, vc, pf, glat, glon, own, spread, pick, lon,
    wide, weighted, halo_out, halo_in, edge, part, cpert, cv, cpart, crecv, zfine, zcoarse,
    load, a_send, a_recv, v_send, v_recv, h_send, h_recv, c_send, c_recv, f_send, f_recv, z_send, z_recv,
):
    mem = lax.axis_index("mem")
    lat = lax.axis_index("lat")
    count, rows, width = pert_fine.shape
    crows, cwidth = v_coarse.shape
    mine = count // bands
    edges = REACH * count

    loads = [
        pltpu.make_async_copy(src, dst, load.at[i])
        for i, (src, dst) in enumerate(
            [
                (v_coarse, vc),
                (pert_fine, pf),
                (v_fine, vf),
                (spread_m, spread),
                (lon_m, lon),
                (own_m, own),
                (pick_m, pick),
                (gauss_lon, glon),
                (gauss_lat, glat),
                (pert_coarse.at[pl.ds(lat * mine, mine)], cpert.at[lat]),
            ]
        )
    ]
    for copy in loads:
        copy.start()

    def peer_lat(o):
        return lax.rem(lat + o, bands)

    def peer_mem(o):
        return lax.rem(mem + o, groups)

    barrier = pltpu.get_barrier_semaphore()
    for o in range(1, bands):
        pl.semaphore_signal(barrier, inc=1, device_id=(mem, peer_lat(o)), device_id_type=MESH)
    for o in range(1, groups):
        pl.semaphore_signal(barrier, inc=1, device_id=(peer_mem(o), lat), device_id_type=MESH)
    pl.semaphore_wait(barrier, bands - 1 + groups - 1)

    def over_lat(o, src, dst, send, recv):
        return pltpu.make_async_remote_copy(
            src_ref=src, dst_ref=dst.at[lat], send_sem=send.at[o - 1], recv_sem=recv.at[lat],
            device_id=(mem, peer_lat(o)), device_id_type=MESH,
        )

    def from_lat(o, dst, send, recv):
        at = lax.rem(lat + bands - o, bands)
        pltpu.make_async_remote_copy(
            src_ref=dst.at[at], dst_ref=dst.at[at], send_sem=send.at[o - 1], recv_sem=recv.at[at],
            device_id=(mem, peer_lat(o)), device_id_type=MESH,
        ).wait_recv()

    def over_mem(o, ref, send, recv):
        return pltpu.make_async_remote_copy(
            src_ref=ref.at[mem], dst_ref=ref.at[mem], send_sem=send.at[o - 1], recv_sem=recv.at[mem],
            device_id=(peer_mem(o), lat), device_id_type=MESH,
        )

    def from_mem(o, ref, send, recv):
        at = lax.rem(mem + groups - o, groups)
        pltpu.make_async_remote_copy(
            src_ref=ref.at[at], dst_ref=ref.at[at], send_sem=send.at[o - 1], recv_sem=recv.at[at],
            device_id=(peer_mem(o), lat), device_id_type=MESH,
        ).wait_recv()

    sent = []

    for o in range(1, bands):
        copy = over_lat(o, pert_coarse.at[pl.ds(peer_lat(o) * mine, mine)], cpert, a_send, a_recv)
        copy.start()
        sent.append(copy)
    loads[0].wait()
    cv[lat] = vc[...].astype(BF16)
    for o in range(1, bands):
        copy = over_lat(o, cv.at[lat], cv, v_send, v_recv)
        copy.start()
        sent.append(copy)

    for copy in loads[1:5]:
        copy.wait()
    weighted[...] = (pf[...].astype(F32) * vf[...][None]).astype(BF16).reshape(count * rows, width)
    half = block // 2

    def smooth(matrix, n):
        along = dot(matrix, weighted[...]).astype(BF16)
        wide[0:n, half : half + width] = along
        wide[0:n, 0:half] = along[:, width - half :]
        wide[0:n, half + width :] = along[:, :half]
        for b in range(width // block):
            yield b * block, dot(wide[0:n, b * block : (b + 2) * block], lon[...])

    for at, value in smooth(spread[...], 2 * edges):
        halo_out[:, :, at : at + block] = value.astype(BF16).reshape(2, edges, block)

    def halo(side, target):
        return pltpu.make_async_remote_copy(
            src_ref=halo_out.at[side], dst_ref=halo_in.at[side],
            send_sem=h_send.at[side], recv_sem=h_recv.at[side],
            device_id=(mem, target), device_id_type=MESH,
        )

    @pl.when(lat < bands - 1)
    def _():
        halo(0, lat + 1).start()

    @pl.when(lat > 0)
    def _():
        halo(1, lat - 1).start()

    loads[5].wait()
    for at, value in smooth(own[...], count * rows):
        product = value.reshape(count, rows, block) * pf[:, :, at : at + block].astype(F32)
        part[:, at : at + block] = jnp.sum(product, axis=0)
    loads[6].wait()
    edge[...] = dot(pick[...], pf[...].reshape(count * rows, width)).astype(BF16).reshape(2, edges, width)

    for copy in loads[7:]:
        copy.wait()
    for o in range(1, bands):
        from_lat(o, cpert, a_send, a_recv)
    for o in range(1, bands):
        from_lat(o, cv, v_send, v_recv)
    total = jnp.zeros((bands * crows, cwidth), F32)
    for j in range(mine):
        pert = cpert[:, j].astype(F32).reshape(bands * crows, cwidth)
        value = (pert * cv[...].astype(F32).reshape(bands * crows, cwidth)).astype(BF16)
        value = lax.dot_general(value, glon[...], (((1,), (1,)), ((), ())), preferred_element_type=F32)
        value = dot(glat[...], value.astype(BF16)).astype(BF16)
        total = total + pert * value.astype(F32)
    cpart[...] = total.astype(BF16).reshape(bands, crows, cwidth)
    for o in range(1, bands):
        copy = over_lat(o, cpart.at[peer_lat(o)], crecv, c_send, c_recv)
        copy.start()
        sent.append(copy)
    crecv[lat] = cpart[lat]

    @pl.when(lat > 0)
    def _():
        halo(0, lat - 1).wait_recv()
        product = halo_in[0].astype(F32) * edge[0].astype(F32)
        part[0:REACH] = part[0:REACH] + jnp.sum(product.reshape(REACH, count, width), axis=1)

    @pl.when(lat < bands - 1)
    def _():
        halo(1, lat + 1).wait_recv()
        product = halo_in[1].astype(F32) * edge[1].astype(F32)
        part[rows - REACH :] = part[rows - REACH :] + jnp.sum(product.reshape(REACH, count, width), axis=1)

    zfine[mem] = part[...].astype(BF16)
    for o in range(1, groups):
        copy = over_mem(o, zfine, f_send, f_recv)
        copy.start()
        sent.append(copy)

    for o in range(1, bands):
        from_lat(o, crecv, c_send, c_recv)
    zcoarse[mem] = jnp.sum(crecv[...].astype(F32), axis=0).astype(BF16)
    for o in range(1, groups):
        copy = over_mem(o, zcoarse, z_send, z_recv)
        copy.start()
        sent.append(copy)

    for o in range(1, groups):
        from_mem(o, zfine, f_send, f_recv)
    out_fine[...] = jnp.sum(zfine[...].astype(F32), axis=0) * factor
    for o in range(1, groups):
        from_mem(o, zcoarse, z_send, z_recv)
    out_coarse[...] = jnp.sum(zcoarse[...].astype(F32), axis=0) * factor

    for copy in sent:
        copy.wait_send()

    @pl.when(lat < bands - 1)
    def _():
        halo(0, lat + 1).wait_send()

    @pl.when(lat > 0)
    def _():
        halo(1, lat - 1).wait_send()


def fused(v_fine, v_coarse, pert_fine, pert_coarse, gauss_lat, gauss_lon):
    bands, groups = lax.axis_size("lat"), lax.axis_size("mem")
    count, rows, width = pert_fine.shape
    crows, cwidth = v_coarse.shape
    mine = count // bands
    edges = REACH * count
    block = 256
    half = block // 2
    mats = constants(count, rows, block)
    dma = pltpu.SemaphoreType.DMA
    vmem = pltpu.VMEM
    return pl.pallas_call(
        functools.partial(kernel, bands, groups, block, 1.0 / (count * groups - 1)),
        out_shape=(
            jax.ShapeDtypeStruct((rows, width), F32),
            jax.ShapeDtypeStruct((crows, cwidth), F32),
        ),
        in_specs=[pl.BlockSpec(memory_space=pl.ANY)] * 10,
        out_specs=[pl.BlockSpec(memory_space=pltpu.VMEM)] * 2,
        scratch_shapes=[
            vmem(v_fine.shape, F32),
            vmem(v_coarse.shape, F32),
            vmem(pert_fine.shape, BF16),
            vmem(gauss_lat.shape, BF16),
            vmem(gauss_lon.shape, BF16),
            *[vmem(a.shape, BF16) for a in mats],
            vmem((max(count * rows, 2 * edges), width + 2 * half), BF16),
            vmem((count * rows, width), BF16),
            vmem((2, edges, width), BF16),
            vmem((2, edges, width), BF16),
            vmem((2, edges, width), BF16),
            vmem((rows, width), F32),
            vmem((bands, mine, crows, cwidth), BF16),
            vmem((bands, crows, cwidth), BF16),
            vmem((bands, crows, cwidth), BF16),
            vmem((bands, crows, cwidth), BF16),
            vmem((groups, rows, width), BF16),
            vmem((groups, crows, cwidth), BF16),
            dma((10,)),
            dma((bands,)), dma((bands,)),
            dma((bands,)), dma((bands,)),
            dma((2,)), dma((2,)),
            dma((bands,)), dma((bands,)),
            dma((groups,)), dma((groups,)),
            dma((groups,)), dma((groups,)),
        ],
        compiler_params=pltpu.CompilerParams(
            collective_id=0, has_side_effects=True, vmem_limit_bytes=60 * 1024 * 1024
        ),
        name="covariance",
    )(v_fine, v_coarse, pert_fine, pert_coarse, gauss_lat, gauss_lon, *mats)


def solution(mesh):
    bands = mesh.shape["lat"]
    groups = mesh.shape["mem"]

    def local(v_fine, v_coarse, pert_fine, pert_coarse, gauss_lat, gauss_lon):
        count, rows, width = pert_fine.shape
        crows, cwidth = v_coarse.shape
        even = count % bands == 0 and count % 16 == 0 and crows % 16 == 0 and cwidth % 128 == 0
        if bands > 1 and groups > 1 and even and rows % 16 == 0 and width % 256 == 0:
            return fused(v_fine, v_coarse, pert_fine, pert_coarse, gauss_lat, gauss_lon)
        return general(v_fine, v_coarse, pert_fine, pert_coarse, gauss_lat, gauss_lon)

    placed = (
        P("lat", None),
        P("lat", None),
        P("mem", "lat", None),
        P("mem", "lat", None),
        P(),
        P(),
    )
    return jax.shard_map(
        local,
        mesh=mesh,
        in_specs=placed,
        out_specs=(P("lat", None), P("lat", None)),
        check_vma=False,
    )
```

```python
import functools
import math

import jax
import jax.numpy as jnp
import numpy as np
from jax import lax
from jax.experimental import pallas as pl
from jax.experimental.pallas import tpu as pltpu
from jax.sharding import PartitionSpec as P

REACH = 5
MESH = pl.DeviceIdType.MESH
F32 = jnp.float32
BF16 = jnp.bfloat16


def extended(shard, sides, width):
    for axis, dim in sides:
        count, length = (lax.axis_size(axis), shard.shape[dim])
        up = [(i, (i + 1) % count) for i in range(count - 1)]
        down = [(j, i) for i, j in up]
        last = lax.slice_in_dim(shard, length - width, length, axis=dim)
        leading = lax.slice_in_dim(shard, 0, width, axis=dim)
        before = lax.ppermute(last, axis, up)
        after = lax.ppermute(leading, axis, down)
        shard = jnp.concatenate([before, shard, after], axis=dim)
    return shard


def fine_taps():
    return [math.exp(-(offset - 5) * (offset - 5) / 32.0) for offset in range(11)]


def general(v_fine, v_coarse, pert_fine, pert_coarse, gauss_lat, gauss_lon):
    taps = fine_taps()
    count = pert_fine.shape[0]
    members = count * lax.axis_size("mem")
    rows = pert_fine.shape[1]
    weighted = (pert_fine.astype(jnp.float32) * v_fine[None]).astype(jnp.bfloat16)
    padded = extended(weighted, (("lat", 1),), 5)
    along = taps[0] * padded[:, 0:rows].astype(jnp.float32)
    for offset in range(1, 11):
        along = along + taps[offset] * padded[:, offset : offset + rows].astype(jnp.float32)
    across = taps[0] * jnp.roll(along, -5, axis=2)
    for offset in range(1, 11):
        across = across + taps[offset] * jnp.roll(along, offset - 5, axis=2)
    fine_part = jnp.sum(pert_fine.astype(jnp.float32) * across, axis=0)
    crows = pert_coarse.shape[1]
    cwidth = pert_coarse.shape[2]
    cweighted = (pert_coarse.astype(jnp.float32) * v_coarse[None]).astype(jnp.bfloat16)
    flat_rows = cweighted.reshape(count * crows, cwidth)
    ctrans = jnp.einsum("rc,dc->rd", flat_rows, gauss_lon, preferred_element_type=jnp.float32)
    ctrans = ctrans.astype(jnp.bfloat16).reshape(count, crows, cwidth)
    band = lax.dynamic_slice_in_dim(gauss_lat, lax.axis_index("lat") * crows, crows, 0)
    smooth = jnp.einsum(
        "rj,mjc->mrc",
        band,
        lax.all_gather(ctrans, "lat", axis=1, tiled=True),
        preferred_element_type=jnp.float32,
    ).astype(jnp.bfloat16)
    coarse_part = jnp.sum(pert_coarse.astype(jnp.float32) * smooth.astype(jnp.float32), axis=0)
    fine_total, coarse_total = lax.psum((fine_part, coarse_part), "mem")
    factor = 1.0 / (members - 1)
    return (fine_total * factor, coarse_total * factor)


def tap(d):
    return np.where(np.abs(d) <= REACH, np.exp(-(d * d) / 32.0), 0.0)


def constants(count, rows, block):
    member = np.repeat(np.arange(count), rows)
    row = np.tile(np.arange(rows), count)
    own = (member[:, None] == member[None, :]) * tap(row[:, None] - row[None, :])
    edge_member = np.tile(np.arange(count), REACH)
    step = np.repeat(np.arange(REACH), count)
    same = edge_member[:, None] == member[None, :]
    to_next = same * tap(row[None, :] - (rows + step)[:, None])
    to_before = same * tap(row[None, :] - (step - REACH)[:, None])
    first = same * (row[None, :] == step[:, None])
    last = same * (row[None, :] == (rows - REACH + step)[:, None])
    half = block // 2
    lon = tap(np.arange(2 * block)[:, None] - half - np.arange(block)[None, :])
    spread = np.concatenate([to_next, to_before], 0)
    pick = np.concatenate([first, last], 0)
    return [jnp.asarray(a, BF16) for a in (own, spread, pick, lon)]


def dot(a, b):
    return jnp.dot(a, b, preferred_element_type=F32)


def kernel(
    bands, groups, block, factor,
    v_fine, v_coarse, pert_fine, pert_coarse, gauss_lat, gauss_lon, own_m, spread_m, pick_m, lon_m,
    out_fine, out_coarse,
    vf, vc, pf, glat, glon, own, spread, pick, lon,
    wide, weighted, halo_out, halo_in, edge, part, pc, cout, cin, sout, sin, zfine, zcoarse,
    load, a_send, a_recv, h_send, h_recv, c_send, c_recv, f_send, f_recv, z_send, z_recv,
):
    mem = lax.axis_index("mem")
    lat = lax.axis_index("lat")
    count, rows, width = pert_fine.shape
    crows, cwidth = v_coarse.shape
    mine = count // bands
    edges = REACH * count

    loads = [
        pltpu.make_async_copy(src, dst, load.at[i])
        for i, (src, dst) in enumerate(
            [
                (v_coarse, vc),
                (pert_coarse, pc),
                (pert_fine, pf),
                (v_fine, vf),
                (spread_m, spread),
                (lon_m, lon),
                (own_m, own),
                (pick_m, pick),
                (gauss_lon, glon),
                (gauss_lat, glat),
            ]
        )
    ]
    for copy in loads:
        copy.start()

    def peer_lat(o):
        return lax.rem(lat + o, bands)

    def peer_mem(o):
        return lax.rem(mem + o, groups)

    barrier = pltpu.get_barrier_semaphore()
    for o in range(1, bands):
        pl.semaphore_signal(barrier, inc=1, device_id=(mem, peer_lat(o)), device_id_type=MESH)
    for o in range(1, groups):
        pl.semaphore_signal(barrier, inc=1, device_id=(peer_mem(o), lat), device_id_type=MESH)
    pl.semaphore_wait(barrier, bands - 1 + groups - 1)

    def over_lat(o, src, dst, send, recv):
        return pltpu.make_async_remote_copy(
            src_ref=src, dst_ref=dst.at[lat], send_sem=send.at[o - 1], recv_sem=recv.at[lat],
            device_id=(mem, peer_lat(o)), device_id_type=MESH,
        )

    def from_lat(o, dst, send, recv):
        at = lax.rem(lat + bands - o, bands)
        pltpu.make_async_remote_copy(
            src_ref=dst.at[at], dst_ref=dst.at[at], send_sem=send.at[o - 1], recv_sem=recv.at[at],
            device_id=(mem, peer_lat(o)), device_id_type=MESH,
        ).wait_recv()

    def over_mem(o, ref, send, recv):
        return pltpu.make_async_remote_copy(
            src_ref=ref.at[mem], dst_ref=ref.at[mem], send_sem=send.at[o - 1], recv_sem=recv.at[mem],
            device_id=(peer_mem(o), lat), device_id_type=MESH,
        )

    def from_mem(o, ref, send, recv):
        at = lax.rem(mem + groups - o, groups)
        pltpu.make_async_remote_copy(
            src_ref=ref.at[at], dst_ref=ref.at[at], send_sem=send.at[o - 1], recv_sem=recv.at[at],
            device_id=(peer_mem(o), lat), device_id_type=MESH,
        ).wait_recv()

    sent = []

    for copy in loads[:2]:
        copy.wait()
    cweighted = (pc[...].astype(F32) * vc[...][None]).astype(BF16)
    cout[...] = cweighted.reshape(bands, mine, crows, cwidth)
    for o in range(1, bands):
        copy = over_lat(o, cout.at[peer_lat(o)], cin, a_send, a_recv)
        copy.start()
        sent.append(copy)
    cin[lat] = cout[lat]

    for copy in loads[2:6]:
        copy.wait()
    weighted[...] = (pf[...].astype(F32) * vf[...][None]).astype(BF16).reshape(count * rows, width)
    half = block // 2

    def smooth(matrix, n):
        along = dot(matrix, weighted[...]).astype(BF16)
        wide[0:n, half : half + width] = along
        wide[0:n, 0:half] = along[:, width - half :]
        wide[0:n, half + width :] = along[:, :half]
        for b in range(width // block):
            yield b * block, dot(wide[0:n, b * block : (b + 2) * block], lon[...])

    for at, value in smooth(spread[...], 2 * edges):
        halo_out[:, :, at : at + block] = value.astype(BF16).reshape(2, edges, block)

    def halo(side, target):
        return pltpu.make_async_remote_copy(
            src_ref=halo_out.at[side], dst_ref=halo_in.at[side],
            send_sem=h_send.at[side], recv_sem=h_recv.at[side],
            device_id=(mem, target), device_id_type=MESH,
        )

    @pl.when(lat < bands - 1)
    def _():
        halo(0, lat + 1).start()

    @pl.when(lat > 0)
    def _():
        halo(1, lat - 1).start()

    loads[6].wait()
    for at, value in smooth(own[...], count * rows):
        product = value.reshape(count, rows, block) * pf[:, :, at : at + block].astype(F32)
        part[:, at : at + block] = jnp.sum(product, axis=0)
    loads[7].wait()
    edge[...] = dot(pick[...], pf[...].reshape(count * rows, width)).astype(BF16).reshape(2, edges, width)

    for copy in loads[8:]:
        copy.wait()
    for o in range(1, bands):
        from_lat(o, cin, a_send, a_recv)
    for j in range(mine):
        value = cin[:, j].reshape(bands * crows, cwidth)
        value = lax.dot_general(value, glon[...], (((1,), (1,)), ((), ())), preferred_element_type=F32)
        value = dot(glat[...], value.astype(BF16)).astype(BF16)
        sout[:, j] = value.reshape(bands, crows, cwidth)
    for o in range(1, bands):
        copy = over_lat(o, sout.at[peer_lat(o)], sin, c_send, c_recv)
        copy.start()
        sent.append(copy)
    sin[lat] = sout[lat]

    @pl.when(lat > 0)
    def _():
        halo(0, lat - 1).wait_recv()
        product = halo_in[0].astype(F32) * edge[0].astype(F32)
        part[0:REACH] = part[0:REACH] + jnp.sum(product.reshape(REACH, count, width), axis=1)

    @pl.when(lat < bands - 1)
    def _():
        halo(1, lat + 1).wait_recv()
        product = halo_in[1].astype(F32) * edge[1].astype(F32)
        part[rows - REACH :] = part[rows - REACH :] + jnp.sum(product.reshape(REACH, count, width), axis=1)

    zfine[mem] = part[...].astype(BF16)
    for o in range(1, groups):
        copy = over_mem(o, zfine, f_send, f_recv)
        copy.start()
        sent.append(copy)

    for o in range(1, bands):
        from_lat(o, sin, c_send, c_recv)
    smoothed = sin[...].reshape(count, crows, cwidth).astype(F32)
    zcoarse[mem] = jnp.sum(pc[...].astype(F32) * smoothed, axis=0).astype(BF16)
    for o in range(1, groups):
        copy = over_mem(o, zcoarse, z_send, z_recv)
        copy.start()
        sent.append(copy)

    for o in range(1, groups):
        from_mem(o, zfine, f_send, f_recv)
    out_fine[...] = jnp.sum(zfine[...].astype(F32), axis=0) * factor
    for o in range(1, groups):
        from_mem(o, zcoarse, z_send, z_recv)
    out_coarse[...] = jnp.sum(zcoarse[...].astype(F32), axis=0) * factor

    for copy in sent:
        copy.wait_send()

    @pl.when(lat < bands - 1)
    def _():
        halo(0, lat + 1).wait_send()

    @pl.when(lat > 0)
    def _():
        halo(1, lat - 1).wait_send()


def fused(v_fine, v_coarse, pert_fine, pert_coarse, gauss_lat, gauss_lon):
    bands, groups = lax.axis_size("lat"), lax.axis_size("mem")
    count, rows, width = pert_fine.shape
    crows, cwidth = v_coarse.shape
    mine = count // bands
    edges = REACH * count
    block = 256
    half = block // 2
    mats = constants(count, rows, block)
    dma = pltpu.SemaphoreType.DMA
    vmem = pltpu.VMEM
    return pl.pallas_call(
        functools.partial(kernel, bands, groups, block, 1.0 / (count * groups - 1)),
        out_shape=(
            jax.ShapeDtypeStruct((rows, width), F32),
            jax.ShapeDtypeStruct((crows, cwidth), F32),
        ),
        in_specs=[pl.BlockSpec(memory_space=pl.ANY)] * 10,
        out_specs=[pl.BlockSpec(memory_space=pltpu.VMEM)] * 2,
        scratch_shapes=[
            vmem(v_fine.shape, F32),
            vmem(v_coarse.shape, F32),
            vmem(pert_fine.shape, BF16),
            vmem(gauss_lat.shape, BF16),
            vmem(gauss_lon.shape, BF16),
            *[vmem(a.shape, BF16) for a in mats],
            vmem((max(count * rows, 2 * edges), width + 2 * half), BF16),
            vmem((count * rows, width), BF16),
            vmem((2, edges, width), BF16),
            vmem((2, edges, width), BF16),
            vmem((2, edges, width), BF16),
            vmem((rows, width), F32),
            vmem(pert_coarse.shape, BF16),
            *[vmem((bands, mine, crows, cwidth), BF16)] * 4,
            vmem((groups, rows, width), BF16),
            vmem((groups, crows, cwidth), BF16),
            dma((10,)),
            dma((bands,)), dma((bands,)),
            dma((2,)), dma((2,)),
            dma((bands,)), dma((bands,)),
            dma((groups,)), dma((groups,)),
            dma((groups,)), dma((groups,)),
        ],
        compiler_params=pltpu.CompilerParams(
            collective_id=0, has_side_effects=True, vmem_limit_bytes=60 * 1024 * 1024
        ),
        name="covariance",
    )(v_fine, v_coarse, pert_fine, pert_coarse, gauss_lat, gauss_lon, *mats)


def solution(mesh):
    bands = mesh.shape["lat"]
    groups = mesh.shape["mem"]

    def local(v_fine, v_coarse, pert_fine, pert_coarse, gauss_lat, gauss_lon):
        count, rows, width = pert_fine.shape
        crows, cwidth = v_coarse.shape
        even = count % bands == 0 and count % 16 == 0 and crows % 16 == 0 and cwidth % 128 == 0
        if bands > 1 and groups > 1 and even and rows % 16 == 0 and width % 256 == 0:
            return fused(v_fine, v_coarse, pert_fine, pert_coarse, gauss_lat, gauss_lon)
        return general(v_fine, v_coarse, pert_fine, pert_coarse, gauss_lat, gauss_lon)

    placed = (
        P("lat", None),
        P("lat", None),
        P("mem", "lat", None),
        P("mem", "lat", None),
        P(),
        P(),
    )
    return jax.shard_map(
        local,
        mesh=mesh,
        in_specs=placed,
        out_specs=(P("lat", None), P("lat", None)),
        check_vma=False,
    )
```

```python
import functools
import math

import jax
import jax.numpy as jnp
import numpy as np
from jax import lax
from jax.experimental import pallas as pl
from jax.experimental.pallas import tpu as pltpu
from jax.sharding import PartitionSpec as P

REACH = 5
MESH = pl.DeviceIdType.MESH
F32 = jnp.float32
BF16 = jnp.bfloat16


def extended(shard, sides, width):
    for axis, dim in sides:
        count, length = (lax.axis_size(axis), shard.shape[dim])
        up = [(i, (i + 1) % count) for i in range(count - 1)]
        down = [(j, i) for i, j in up]
        last = lax.slice_in_dim(shard, length - width, length, axis=dim)
        leading = lax.slice_in_dim(shard, 0, width, axis=dim)
        before = lax.ppermute(last, axis, up)
        after = lax.ppermute(leading, axis, down)
        shard = jnp.concatenate([before, shard, after], axis=dim)
    return shard


def fine_taps():
    return [math.exp(-(offset - 5) * (offset - 5) / 32.0) for offset in range(11)]


def general(v_fine, v_coarse, pert_fine, pert_coarse, gauss_lat, gauss_lon):
    taps = fine_taps()
    count = pert_fine.shape[0]
    members = count * lax.axis_size("mem")
    rows = pert_fine.shape[1]
    weighted = (pert_fine.astype(jnp.float32) * v_fine[None]).astype(jnp.bfloat16)
    padded = extended(weighted, (("lat", 1),), 5)
    along = taps[0] * padded[:, 0:rows].astype(jnp.float32)
    for offset in range(1, 11):
        along = along + taps[offset] * padded[:, offset : offset + rows].astype(jnp.float32)
    across = taps[0] * jnp.roll(along, -5, axis=2)
    for offset in range(1, 11):
        across = across + taps[offset] * jnp.roll(along, offset - 5, axis=2)
    fine_part = jnp.sum(pert_fine.astype(jnp.float32) * across, axis=0)
    crows = pert_coarse.shape[1]
    cwidth = pert_coarse.shape[2]
    cweighted = (pert_coarse.astype(jnp.float32) * v_coarse[None]).astype(jnp.bfloat16)
    flat_rows = cweighted.reshape(count * crows, cwidth)
    ctrans = jnp.einsum("rc,dc->rd", flat_rows, gauss_lon, preferred_element_type=jnp.float32)
    ctrans = ctrans.astype(jnp.bfloat16).reshape(count, crows, cwidth)
    band = lax.dynamic_slice_in_dim(gauss_lat, lax.axis_index("lat") * crows, crows, 0)
    smooth = jnp.einsum(
        "rj,mjc->mrc",
        band,
        lax.all_gather(ctrans, "lat", axis=1, tiled=True),
        preferred_element_type=jnp.float32,
    ).astype(jnp.bfloat16)
    coarse_part = jnp.sum(pert_coarse.astype(jnp.float32) * smooth.astype(jnp.float32), axis=0)
    fine_total, coarse_total = lax.psum((fine_part, coarse_part), "mem")
    factor = 1.0 / (members - 1)
    return (fine_total * factor, coarse_total * factor)


def tap(d):
    return np.where(np.abs(d) <= REACH, np.exp(-(d * d) / 32.0), 0.0)


def constants(count, rows, block):
    member = np.repeat(np.arange(count), rows)
    row = np.tile(np.arange(rows), count)
    own = (member[:, None] == member[None, :]) * tap(row[:, None] - row[None, :])
    edge_member = np.tile(np.arange(count), REACH)
    step = np.repeat(np.arange(REACH), count)
    same = edge_member[:, None] == member[None, :]
    to_next = same * tap(row[None, :] - (rows + step)[:, None])
    to_before = same * tap(row[None, :] - (step - REACH)[:, None])
    first = same * (row[None, :] == step[:, None])
    last = same * (row[None, :] == (rows - REACH + step)[:, None])
    half = block // 2
    lon = tap(np.arange(2 * block)[:, None] - half - np.arange(block)[None, :])
    spread = np.concatenate([to_next, to_before], 0)
    pick = np.concatenate([first, last], 0)
    return [jnp.asarray(a, BF16) for a in (own, spread, pick, lon)]


def dot(a, b):
    return jnp.dot(a, b, preferred_element_type=F32)


def kernel(
    bands, groups, block, factor,
    v_fine, v_coarse, pert_fine, pert_coarse, gauss_lat, gauss_lon, own_m, spread_m, pick_m, lon_m,
    out_fine, out_coarse,
    vf, vc, pf, glat, glon, own, spread, pick, lon,
    wide, weighted, halo_out, halo_in, edge, part, pc, cout, cin, sout, sin, zfine, zcoarse,
    load, a_send, a_recv, h_send, h_recv, c_send, c_recv, f_send, f_recv, z_send, z_recv,
):
    mem = lax.axis_index("mem")
    lat = lax.axis_index("lat")
    count, rows, width = pert_fine.shape
    crows, cwidth = v_coarse.shape
    mine = count // bands
    edges = REACH * count

    loads = [
        pltpu.make_async_copy(src, dst, load.at[i])
        for i, (src, dst) in enumerate(
            [
                (v_coarse, vc),
                (pert_coarse, pc),
                (pert_fine, pf),
                (v_fine, vf),
                (spread_m, spread),
                (lon_m, lon),
                (own_m, own),
                (pick_m, pick),
                (gauss_lon, glon),
                (gauss_lat, glat),
            ]
        )
    ]
    for copy in loads:
        copy.start()

    def peer_lat(o):
        return lax.rem(lat + o, bands)

    def peer_mem(o):
        return lax.rem(mem + o, groups)

    barrier = pltpu.get_barrier_semaphore()
    for o in range(1, bands):
        pl.semaphore_signal(barrier, inc=1, device_id=(mem, peer_lat(o)), device_id_type=MESH)
    for o in range(1, groups):
        pl.semaphore_signal(barrier, inc=1, device_id=(peer_mem(o), lat), device_id_type=MESH)

    for copy in loads[:2]:
        copy.wait()
    for j in range(mine):
        for b in range(bands):
            cout[j, b] = (pc[b * mine + j].astype(F32) * vc[...]).astype(BF16)
    for j in range(mine):
        cin[j, lat] = cout[j, lat]

    pl.semaphore_wait(barrier, bands - 1 + groups - 1)

    def over_lat(j, o, src, dst, send, recv):
        return pltpu.make_async_remote_copy(
            src_ref=src.at[j, peer_lat(o)], dst_ref=dst.at[j, lat],
            send_sem=send.at[j, o - 1], recv_sem=recv.at[j, lat],
            device_id=(mem, peer_lat(o)), device_id_type=MESH,
        )

    def from_lat(j, o, dst, send, recv):
        at = lax.rem(lat + bands - o, bands)
        pltpu.make_async_remote_copy(
            src_ref=dst.at[j, at], dst_ref=dst.at[j, at],
            send_sem=send.at[j, o - 1], recv_sem=recv.at[j, at],
            device_id=(mem, peer_lat(o)), device_id_type=MESH,
        ).wait_recv()
        return at

    def over_mem(o, ref, send, recv):
        return pltpu.make_async_remote_copy(
            src_ref=ref.at[mem], dst_ref=ref.at[mem], send_sem=send.at[o - 1], recv_sem=recv.at[mem],
            device_id=(peer_mem(o), lat), device_id_type=MESH,
        )

    def from_mem(o, ref, send, recv):
        at = lax.rem(mem + groups - o, groups)
        pltpu.make_async_remote_copy(
            src_ref=ref.at[at], dst_ref=ref.at[at], send_sem=send.at[o - 1], recv_sem=recv.at[at],
            device_id=(peer_mem(o), lat), device_id_type=MESH,
        ).wait_recv()

    sent = []

    for j in range(mine):
        for o in range(1, bands):
            copy = over_lat(j, o, cout, cin, a_send, a_recv)
            copy.start()
            sent.append(copy)

    for copy in loads[2:6]:
        copy.wait()
    weighted[...] = (pf[...].astype(F32) * vf[...][None]).astype(BF16).reshape(count * rows, width)
    half = block // 2

    def smooth(matrix, n):
        along = dot(matrix, weighted[...]).astype(BF16)
        wide[0:n, half : half + width] = along
        wide[0:n, 0:half] = along[:, width - half :]
        wide[0:n, half + width :] = along[:, :half]
        for b in range(width // block):
            yield b * block, dot(wide[0:n, b * block : (b + 2) * block], lon[...])

    for at, value in smooth(spread[...], 2 * edges):
        halo_out[:, :, at : at + block] = value.astype(BF16).reshape(2, edges, block)

    def halo(side, target):
        return pltpu.make_async_remote_copy(
            src_ref=halo_out.at[side], dst_ref=halo_in.at[side],
            send_sem=h_send.at[side], recv_sem=h_recv.at[side],
            device_id=(mem, target), device_id_type=MESH,
        )

    @pl.when(lat < bands - 1)
    def _():
        halo(0, lat + 1).start()

    @pl.when(lat > 0)
    def _():
        halo(1, lat - 1).start()

    loads[6].wait()
    for at, value in smooth(own[...], count * rows):
        product = value.reshape(count, rows, block) * pf[:, :, at : at + block].astype(F32)
        part[:, at : at + block] = jnp.sum(product, axis=0)
    loads[7].wait()
    edge[...] = dot(pick[...], pf[...].reshape(count * rows, width)).astype(BF16).reshape(2, edges, width)

    for copy in loads[8:]:
        copy.wait()
    for j in range(mine):
        for o in range(1, bands):
            from_lat(j, o, cin, a_send, a_recv)
        value = cin[j].reshape(bands * crows, cwidth)
        value = lax.dot_general(value, glon[...], (((1,), (1,)), ((), ())), preferred_element_type=F32)
        value = dot(glat[...], value.astype(BF16)).astype(BF16)
        sout[j] = value.reshape(bands, crows, cwidth)
        for o in range(1, bands):
            copy = over_lat(j, o, sout, sin, c_send, c_recv)
            copy.start()
            sent.append(copy)

    @pl.when(lat > 0)
    def _():
        halo(0, lat - 1).wait_recv()
        product = halo_in[0].astype(F32) * edge[0].astype(F32)
        part[0:REACH] = part[0:REACH] + jnp.sum(product.reshape(REACH, count, width), axis=1)

    @pl.when(lat < bands - 1)
    def _():
        halo(1, lat + 1).wait_recv()
        product = halo_in[1].astype(F32) * edge[1].astype(F32)
        part[rows - REACH :] = part[rows - REACH :] + jnp.sum(product.reshape(REACH, count, width), axis=1)

    zfine[mem] = part[...].astype(BF16)
    for o in range(1, groups):
        copy = over_mem(o, zfine, f_send, f_recv)
        copy.start()
        sent.append(copy)

    total = jnp.zeros((crows, cwidth), F32)
    for j in range(mine):
        total = total + pc[lat * mine + j].astype(F32) * sout[j, lat].astype(F32)
    for j in range(mine):
        for o in range(1, bands):
            at = from_lat(j, o, sin, c_send, c_recv)
            total = total + pc[at * mine + j].astype(F32) * sin[j, at].astype(F32)
    zcoarse[mem] = total.astype(BF16)
    for o in range(1, groups):
        copy = over_mem(o, zcoarse, z_send, z_recv)
        copy.start()
        sent.append(copy)

    for o in range(1, groups):
        from_mem(o, zfine, f_send, f_recv)
    out_fine[...] = jnp.sum(zfine[...].astype(F32), axis=0) * factor
    for o in range(1, groups):
        from_mem(o, zcoarse, z_send, z_recv)
    out_coarse[...] = jnp.sum(zcoarse[...].astype(F32), axis=0) * factor

    for copy in sent:
        copy.wait_send()

    @pl.when(lat < bands - 1)
    def _():
        halo(0, lat + 1).wait_send()

    @pl.when(lat > 0)
    def _():
        halo(1, lat - 1).wait_send()


def fused(v_fine, v_coarse, pert_fine, pert_coarse, gauss_lat, gauss_lon):
    bands, groups = lax.axis_size("lat"), lax.axis_size("mem")
    count, rows, width = pert_fine.shape
    crows, cwidth = v_coarse.shape
    mine = count // bands
    edges = REACH * count
    block = 256
    half = block // 2
    mats = constants(count, rows, block)
    dma = pltpu.SemaphoreType.DMA
    vmem = pltpu.VMEM
    return pl.pallas_call(
        functools.partial(kernel, bands, groups, block, 1.0 / (count * groups - 1)),
        out_shape=(
            jax.ShapeDtypeStruct((rows, width), F32),
            jax.ShapeDtypeStruct((crows, cwidth), F32),
        ),
        in_specs=[pl.BlockSpec(memory_space=pl.ANY)] * 10,
        out_specs=[pl.BlockSpec(memory_space=pltpu.VMEM)] * 2,
        scratch_shapes=[
            vmem(v_fine.shape, F32),
            vmem(v_coarse.shape, F32),
            vmem(pert_fine.shape, BF16),
            vmem(gauss_lat.shape, BF16),
            vmem(gauss_lon.shape, BF16),
            *[vmem(a.shape, BF16) for a in mats],
            vmem((max(count * rows, 2 * edges), width + 2 * half), BF16),
            vmem((count * rows, width), BF16),
            vmem((2, edges, width), BF16),
            vmem((2, edges, width), BF16),
            vmem((2, edges, width), BF16),
            vmem((rows, width), F32),
            vmem(pert_coarse.shape, BF16),
            *[vmem((mine, bands, crows, cwidth), BF16)] * 4,
            vmem((groups, rows, width), BF16),
            vmem((groups, crows, cwidth), BF16),
            dma((10,)),
            dma((mine, bands)), dma((mine, bands)),
            dma((2,)), dma((2,)),
            dma((mine, bands)), dma((mine, bands)),
            dma((groups,)), dma((groups,)),
            dma((groups,)), dma((groups,)),
        ],
        compiler_params=pltpu.CompilerParams(
            collective_id=0, has_side_effects=True, vmem_limit_bytes=60 * 1024 * 1024
        ),
        name="covariance",
    )(v_fine, v_coarse, pert_fine, pert_coarse, gauss_lat, gauss_lon, *mats)


def solution(mesh):
    bands = mesh.shape["lat"]
    groups = mesh.shape["mem"]

    def local(v_fine, v_coarse, pert_fine, pert_coarse, gauss_lat, gauss_lon):
        count, rows, width = pert_fine.shape
        crows, cwidth = v_coarse.shape
        even = count % bands == 0 and count % 16 == 0 and crows % 16 == 0 and cwidth % 128 == 0
        if bands > 1 and groups > 1 and even and rows % 16 == 0 and width % 256 == 0:
            return fused(v_fine, v_coarse, pert_fine, pert_coarse, gauss_lat, gauss_lon)
        return general(v_fine, v_coarse, pert_fine, pert_coarse, gauss_lat, gauss_lon)

    placed = (
        P("lat", None),
        P("lat", None),
        P("mem", "lat", None),
        P("mem", "lat", None),
        P(),
        P(),
    )
    return jax.shard_map(
        local,
        mesh=mesh,
        in_specs=placed,
        out_specs=(P("lat", None), P("lat", None)),
        check_vma=False,
    )
```
